128 devices in a mesh: seq: 32 (over z_hi, x, y), head: 4 (over z_lo, core).
Axes of the slice: x: 4, y: 4, z: 4 (z_hi: 2, z_lo: 2; z = z_hi * 2 + z_lo), core: 2. Of those that a mesh axis runs over, the one named last changes fastest.
Arguments:
- queries: bfloat16 [65536, 2048], P('seq', 'head'), may hold values from -5 to 5
- key_field: bfloat16 [65536, 2048], P('seq', 'head'), may hold values from -5 to 5
- value_field: bfloat16 [65536, 2048], P('seq', 'head'), may hold values from -6 to 6
- out_grad: bfloat16 [65536, 2048], P('seq', 'head'), may hold values from -96 to 96
- prefix_keys: bfloat16 [64, 2048], P(None, 'head'), may hold values from -5 to 5
- prefix_values: bfloat16 [64, 2048], P(None, 'head'), may hold values from -6 to 6
Outputs:
- query_grad: bfloat16 [65536, 2048], P('seq', 'head')
- key_grad: bfloat16 [65536, 2048], P('seq', 'head')
- value_grad: bfloat16 [65536, 2048], P('seq', 'head')
- prefix_key_grad: float32 [64, 2048], P(None, 'head')
- prefix_value_grad: float32 [64, 2048], P(None, 'head')
The draws below stay inside these ranges and needn't reach their ends.
All inputs are finite; a program needn't handle non-finite values.
Results may differ from the reference program's by a relative error of at most 0.0086.
Values may be sent and summed in bfloat16 or wider, within the bound.
A program may use at most 128 MiB of HBM per device.

```python
import math
import jax
import jax.numpy as jnp
from jax import lax

H = 16
DH = 128
C = 1024
NPRE = 64
ROWS = 64
SAMPLES = 65536


def draw_queries(key, part):
    key = jax.random.fold_in(key, 1)
    field = jnp.clip(jax.random.normal(key, (SAMPLES, H * DH), jnp.float32), -5.0, 5.0)
    return field.astype(jnp.bfloat16)


def draw_key_field(key, part):
    key = jax.random.fold_in(key, 2)
    field = jnp.clip(jax.random.normal(key, (SAMPLES, H * DH), jnp.float32), -5.0, 5.0)
    return field.astype(jnp.bfloat16)


def draw_prefix_keys(key, part):
    key = jax.random.fold_in(key, 3)
    field = jnp.clip(jax.random.normal(key, (NPRE, H * DH), jnp.float32), -5.0, 5.0)
    return field.astype(jnp.bfloat16)


def steps_of(rng, extent, cuts, low, top_value):
    loudness, own = 1.0, jax.random.fold_in(rng, 6)
    for axis_at, parts in cuts:
        heights = jnp.exp(jax.random.uniform(jax.random.fold_in(own, axis_at), (parts,), jnp.float32, low / len(cuts), top_value / len(cuts)))
        loudness = loudness * jnp.repeat(heights, extent[axis_at] // parts).reshape([-1 if axis == axis_at else 1 for axis in range(len(extent))])
    return loudness


def bell_draw(own_key, shape, scale, bound, shards=(), kind=jnp.bfloat16):
    loudness = steps_of(own_key, shape, shards, -0.22, 0.18) if shards else 1.0
    values = jax.random.normal(own_key, shape, jnp.float32) * scale * loudness
    return jnp.minimum(jnp.maximum(values, -bound), bound).astype(kind)


def setup_inputs(seed: int = 0) -> dict:
    splits = jax.random.split(jax.random.key(seed), 7)
    queries = draw_queries(jax.random.fold_in(splits[6], 71), 0)
    key_field = draw_key_field(jax.random.fold_in(splits[6], 71), 0)
    value_field = bell_draw(splits[2], (SAMPLES, H * DH), 1.0, 6.0, ((0, 32), (1, 4)))
    out_grad = bell_draw(splits[3], (SAMPLES, H * DH), 16.0, 96.0, ((0, 32), (1, 4)))
    prefix_keys = draw_prefix_keys(jax.random.fold_in(splits[6], 71), 0)
    prefix_values = bell_draw(splits[5], (NPRE, H * DH), 1.0, 6.0, ((1, 4),))
    return {"queries": queries, "key_field": key_field, "value_field": value_field, "out_grad": out_grad, "prefix_keys": prefix_keys, "prefix_values": prefix_values}


def attend(query_blk, key_all, value_all, grad_blk, allowed):
    float_type = jnp.float32
    exact = lax.Precision.HIGHEST
    scaling = 1.0 / math.sqrt(query_blk.shape[-1])
    scores = jnp.einsum('qbd,mbd->bqm', query_blk.astype(float_type), key_all.astype(float_type), precision=exact) * scaling
    scores = jnp.where(allowed, scores, -jnp.inf)
    row_max = lax.optimization_barrier(jnp.max(scores, axis=-1, keepdims=True))
    exp_terms = jnp.exp(scores - row_max)
    attn_probs = exp_terms / lax.optimization_barrier(jnp.sum(exp_terms, axis=-1, keepdims=True))
    attn_round = attn_probs.astype(jnp.bfloat16)
    recomputed = jnp.einsum('bqm,mbd->qbd', attn_round.astype(float_type), value_all.astype(float_type), precision=exact)
    delta_row = lax.optimization_barrier(jnp.sum(grad_blk.astype(float_type) * recomputed, axis=-1))
    dprob = jnp.einsum('qbd,mbd->bqm', grad_blk.astype(float_type), value_all.astype(float_type), precision=exact)
    dscore = (scaling * attn_probs * (dprob - jnp.transpose(delta_row)[:, :, None])).astype(jnp.bfloat16)
    query_part = jnp.einsum('bqm,mbd->qbd', dscore.astype(float_type), key_all.astype(float_type), precision=exact)
    key_part = jnp.einsum('bqm,qbd->mbd', dscore.astype(float_type), query_blk.astype(float_type), precision=exact)
    value_part = jnp.einsum('bqm,qbd->mbd', attn_round.astype(float_type), grad_blk.astype(float_type), precision=exact)
    return (query_part, key_part, value_part)

def reference(queries, key_field, value_field, out_grad, prefix_keys, prefix_values):
    half_heads = H // 2

    def split_heads(array, length):
        shaped = array.reshape(length, half_heads, 2, DH)
        return (shaped[:, :, 0], shaped[:, :, 1])
    q_even, q_odd = split_heads(queries, SAMPLES)
    k_even, k_odd = split_heads(key_field, SAMPLES)
    v_even, v_odd = split_heads(value_field, SAMPLES)
    g_even, g_odd = split_heads(out_grad, SAMPLES)
    pk_even, pk_odd = split_heads(prefix_keys, NPRE)
    pv_even, pv_odd = split_heads(prefix_values, NPRE)
    q_blk = min(512, C)
    zero_rows = jnp.zeros((C, half_heads, DH), jnp.bfloat16)
    k_ext = jnp.concatenate([zero_rows, k_even], axis=0)
    v_ext = jnp.concatenate([zero_rows, v_even], axis=0)
    pos_query = jnp.arange(q_blk, dtype=jnp.int32)[:, None]
    pos_key = jnp.arange(q_blk + C, dtype=jnp.int32)[None, :]
    prefix_on = jnp.ones((q_blk, NPRE), dtype=bool)

    def row_step(carry, block_idx):
        acc_k, acc_v, pre_k, pre_v = carry
        blk_start = block_idx * q_blk
        query_blk = lax.dynamic_slice_in_dim(q_even, blk_start, q_blk, 0)
        grad_blk = lax.dynamic_slice_in_dim(g_even, blk_start, q_blk, 0)
        key_blk = lax.dynamic_slice_in_dim(k_ext, blk_start, q_blk + C, 0)
        value_blk = lax.dynamic_slice_in_dim(v_ext, blk_start, q_blk + C, 0)
        window = (pos_key >= pos_query + 1) & (pos_key <= pos_query + C) & (blk_start + pos_key - C >= 0)
        allowed = jnp.concatenate([prefix_on, window], axis=1)
        query_part, key_part, value_part = attend(query_blk, jnp.concatenate([pk_even, key_blk], axis=0), jnp.concatenate([pv_even, value_blk], axis=0), grad_blk, allowed)
        acc_k = lax.dynamic_update_slice_in_dim(acc_k, lax.dynamic_slice_in_dim(acc_k, blk_start, q_blk + C, 0) + key_part[NPRE:], blk_start, 0)
        acc_v = lax.dynamic_update_slice_in_dim(acc_v, lax.dynamic_slice_in_dim(acc_v, blk_start, q_blk + C, 0) + value_part[NPRE:], blk_start, 0)
        return ((acc_k, acc_v, pre_k + key_part[:NPRE], pre_v + value_part[:NPRE]), query_part.astype(jnp.bfloat16))
    acc_zero = jnp.zeros((C + SAMPLES, half_heads, DH), jnp.float32)
    pre_zero = jnp.zeros((NPRE, half_heads, DH), jnp.float32)
    blocks = jnp.arange(SAMPLES // q_blk, dtype=jnp.int32)
    (acc_k, acc_v, pre_k_even, pre_v_even), dq_blocks = lax.scan(row_step, (acc_zero, acc_zero, pre_zero, pre_zero), blocks)
    dq_even = dq_blocks.reshape(SAMPLES, half_heads, DH)
    dk_even = acc_k[C:].astype(jnp.bfloat16)
    dv_even = acc_v[C:].astype(jnp.bfloat16)
    col_blk = min(8, C)
    batch_size = col_blk * half_heads

    def to_grid(array):
        return array.reshape(ROWS, C, half_heads, DH)
    grid_q, grid_k, grid_v, grid_g = (to_grid(q_odd), to_grid(k_odd), to_grid(v_odd), to_grid(g_odd))
    row_ids = jnp.arange(ROWS, dtype=jnp.int32)
    causal = row_ids[None, :] <= row_ids[:, None]
    allowed_col = jnp.concatenate([jnp.ones((ROWS, NPRE), dtype=bool), causal], axis=1)
    pk_wide = jnp.broadcast_to(pk_odd[:, None], (NPRE, col_blk, half_heads, DH)).reshape(NPRE, batch_size, DH)
    pv_wide = jnp.broadcast_to(pv_odd[:, None], (NPRE, col_blk, half_heads, DH)).reshape(NPRE, batch_size, DH)

    def take_cols(array, blk_start):
        return lax.dynamic_slice_in_dim(array, blk_start, col_blk, 1).reshape(ROWS, batch_size, DH)

    def col_step(carry, block_idx):
        pre_k, pre_v = carry
        blk_start = block_idx * col_blk
        query_part, key_part, value_part = attend(take_cols(grid_q, blk_start), jnp.concatenate([pk_wide, take_cols(grid_k, blk_start)], axis=0), jnp.concatenate([pv_wide, take_cols(grid_v, blk_start)], axis=0), take_cols(grid_g, blk_start), allowed_col)
        shape_out = (ROWS, col_blk, half_heads, DH)
        pre_k = pre_k + key_part[:NPRE].reshape(NPRE, col_blk, half_heads, DH).sum(axis=1)
        pre_v = pre_v + value_part[:NPRE].reshape(NPRE, col_blk, half_heads, DH).sum(axis=1)
        outputs = (query_part.reshape(shape_out).astype(jnp.bfloat16), key_part[NPRE:].reshape(shape_out).astype(jnp.bfloat16), value_part[NPRE:].reshape(shape_out).astype(jnp.bfloat16))
        return ((pre_k, pre_v), outputs)
    col_blocks = jnp.arange(C // col_blk, dtype=jnp.int32)
    (pre_k_odd, pre_v_odd), (dq_cols, dk_cols, dv_cols) = lax.scan(col_step, (pre_zero, pre_zero), col_blocks)

    def from_cols(stacked):
        return jnp.moveaxis(stacked, 0, 1).reshape(SAMPLES, half_heads, DH)

    def merge_heads(even_part, odd_part):
        return jnp.stack([even_part, odd_part], axis=2).reshape(even_part.shape[0], H * DH)
    query_grad = merge_heads(dq_even, from_cols(dq_cols))
    key_grad = merge_heads(dk_even, from_cols(dk_cols))
    value_grad = merge_heads(dv_even, from_cols(dv_cols))
    prefix_key_grad = merge_heads(pre_k_even, pre_k_odd)
    prefix_value_grad = merge_heads(pre_v_even, pre_v_odd)
    return (query_grad, key_grad, value_grad, prefix_key_grad, prefix_value_grad)
```

```python
import math

import jax
import jax.numpy as jnp
from jax import lax
from jax.experimental import pallas as pl
from jax.experimental.pallas import tpu as pltpu
from jax.sharding import PartitionSpec as P

DH = 128
C = 1024
NPRE = 64
N = 32
W = C // N
QB = 256
KB = QB + C
SCALE = 1.0 / math.sqrt(DH)
LOG2E = SCALE * math.log2(math.e)
NEG = -1e30
MESH = pl.DeviceIdType.MESH
F32 = jnp.float32
BF16 = jnp.bfloat16

ORDER = [
    (0, 3, 2), (1, 0, 1), (0, 1, 3), (1, 2, 2), (0, 2, 1), (1, 3, 0), (0, 0, 3), (1, 1, 1),
    (1, 0, 0), (0, 2, 3), (1, 3, 2), (0, 1, 0), (1, 2, 1), (0, 3, 1), (1, 1, 3), (0, 0, 2),
    (1, 3, 3), (0, 2, 0), (1, 0, 2), (0, 1, 1), (1, 2, 3), (0, 3, 0), (1, 1, 0), (0, 2, 2),
    (1, 3, 1), (0, 0, 1), (1, 2, 0), (0, 1, 2), (1, 0, 3), (0, 3, 3), (1, 1, 2),
]


def nt(a, b):
    return lax.dot_general(a, b, (((1,), (1,)), ((), ())), preferred_element_type=F32)


def nn(a, b):
    return lax.dot_general(a, b, (((1,), (0,)), ((), ())), preferred_element_type=F32)


def tn(a, b):
    return lax.dot_general(a, b, (((0,), (0,)), ((), ())), preferred_element_type=F32)


def rows(x):
    return x.reshape(x.shape[-3] * W, DH) if x.ndim == 3 else x.reshape(-1, DH)


def softmax_parts(parts, dparts):
    top = parts[0].max(axis=0, keepdims=True)
    for s in parts[1:]:
        top = jnp.maximum(top, s.max(axis=0, keepdims=True))
    exps = [jnp.exp2((s - top) * LOG2E) for s in parts]
    total = sum(e.sum(axis=0, keepdims=True) for e in exps)
    mixed = sum((e * d).sum(axis=0, keepdims=True) for e, d in zip(exps, dparts))
    inv = 1.0 / total
    delta = mixed * inv
    probs = [e * inv for e in exps]
    ds = [p * (d - delta) for p, d in zip(probs, dparts)]
    return probs, ds


def kernel(
    q, k, v, g, pk, pv, dq_o, dk_o, dv_o, pkg_o, pvg_o,
    st, rc, qe, ge, kx, vx, pks, pvs, acck, accv, accp, oq, okk, ov, hs, hr,
    tin, tout, st2, rc2, pgs, prs, pag,
    lsem, ssem, rsem, hssem, hrsem, h2s, h2r, ssem2, rsem2, pss, prr, pas, par, osem,
):
    me = lax.axis_index("seq")
    z, x, y = me // 16, (me // 4) % 4, me % 4
    ids = [((z + dz) % 2) * 16 + ((x + dx) % 4) * 4 + (y + dy) % 4 for dz, dx, dy in ORDER]
    nxt = (me + 1) % N
    prv = (me + N - 1) % N

    def lane(hh):
        return pl.ds(hh * DH, DH)

    stage = []
    n = 0
    for h in range(2):
        for a, ref in enumerate((q, k, v, g)):
            for r in range(2):
                c = pltpu.make_async_copy(
                    ref.at[r, :, :, lane(2 * h + 1)], st.at[h, :, a, r], lsem.at[n]
                )
                c.start()
                stage.append(c)
                n += 1
    even = []
    for h in range(2):
        for ref, dst in ((k, kx), (v, vx), (q, qe), (g, ge)):
            off = 1 if ref is k or ref is v else 0
            for r in range(2):
                c = pltpu.make_async_copy(
                    ref.at[r, :, :, lane(2 * h)], dst.at[h, r + off], lsem.at[n]
                )
                c.start()
                even.append(c)
                n += 1

    bar = pltpu.get_barrier_semaphore()
    for i in ids:
        pl.semaphore_signal(bar, inc=1, device_id={"seq": i}, device_id_type=MESH)
    for hh in range(4):
        pks[hh] = pk[:, hh * DH : (hh + 1) * DH]
        pvs[hh] = pv[:, hh * DH : (hh + 1) * DH]
    acck[...] = jnp.zeros_like(acck)
    accv[...] = jnp.zeros_like(accv)
    accp[...] = jnp.zeros_like(accp)
    pl.semaphore_wait(bar, N - 1)

    def remote(src, dst, s, r, to):
        c = pltpu.make_async_remote_copy(
            src_ref=src, dst_ref=dst, send_sem=s, recv_sem=r,
            device_id={"seq": to}, device_id_type=MESH,
        )
        c.start()
        return c

    for c in even:
        c.wait()
    halo = []
    for h in range(2):
        for a, ref in enumerate((kx, vx)):
            halo.append(
                remote(ref.at[h, 2], ref.at[h, 0], hssem.at[2 * h + a], hrsem.at[2 * h + a], nxt)
            )
    for c in stage:
        c.wait()
    sent = [[], []]
    for h in range(2):
        for j, to in enumerate(ids):
            sent[h].append(
                remote(st.at[h, to], rc.at[h, me], ssem.at[h, j], rsem.at[h, j], to)
            )

    key_at = lax.broadcasted_iota(jnp.int32, (QB, QB), 0)
    query_at = lax.broadcasted_iota(jnp.int32, (QB, QB), 1)
    causal = key_at <= query_at

    def even_block(h, i):
        qb = rows(qe[h, i // 4, pl.ds((i % 4) * 8, 8)])
        gb = rows(ge[h, i // 4, pl.ds((i % 4) * 8, 8)])

        def window(ref, j):
            at = i + j
            return rows(ref[h, at // 4, pl.ds((at % 4) * 8, 8)])

        ks = [window(kx, j) for j in range(5)]
        vs = [window(vx, j) for j in range(5)]
        pkh, pvh = pks[2 * h], pvs[2 * h]
        s = [nt(kk, qb) for kk in ks]
        for j in range(4):
            s[j] = s[j] + jnp.where((me == 0) & (i + j < 4), NEG, 0.0).astype(F32)
        d = [nt(vv, gb) for vv in vs]
        s0 = jnp.where(causal, s[4], s[0])
        d0 = jnp.where(causal, d[4], d[0])
        probs, ds = softmax_parts(
            [nt(pkh, qb), s0, s[1], s[2], s[3]], [nt(pvh, gb), d0, d[1], d[2], d[3]]
        )

        def spread(parts):
            pre, edge, mid = parts[0], parts[1], parts[2:]
            zero = jnp.zeros_like(edge)
            out = [jnp.where(causal, zero, edge), *mid, jnp.where(causal, edge, zero)]
            return pre.astype(BF16), [o.astype(BF16) for o in out]

        p_pre, p = spread(probs)
        ds_pre, dd = spread(ds)
        dq = tn(pkh, ds_pre)
        for j in range(5):
            at = pl.ds((i + j) * QB, QB)
            accv[h, at] += nn(p[j], gb)
            acck[h, at] += nn(dd[j], qb)
            dq = dq + tn(ks[j], dd[j])
        accp[0, 2 * h] += nn(ds_pre, qb)
        accp[1, 2 * h] += nn(p_pre, gb)
        oq[h, i // 4, pl.ds((i % 4) * 8, 8)] = (
            (jnp.transpose(dq) * SCALE).astype(BF16).reshape(QB // W, W, DH)
        )

    @pl.loop(0, 8)
    def _(step):
        even_block(step // 4, step % 4 + 4)

    for c in halo:
        c.wait_recv()

    @pl.loop(0, 8)
    def _(step):
        even_block(step // 4, step % 4)

    back = []
    for h in range(2):
        hs[h, 0] = (acck[h, :C] * SCALE).astype(BF16)
        hs[h, 1] = accv[h, :C].astype(BF16)
        back.append(remote(hs.at[h], hr.at[h], h2s.at[h], h2r.at[h], prv))

    key_col = key_at // 64
    query_col = query_at // 64
    column = (key_col == query_col) & (key_at % 64 <= query_at % 64)

    def odd_head(h):
        for a in range(4):
            @pl.loop(0, N)
            def _(b):
                tin[a, pl.ds(b * 64, 64)] = rows(rc[h, b, a]).astype(F32)

        pkh, pvh = pks[2 * h + 1], pvs[2 * h + 1]

        @pl.loop(0, W // 4)
        def _(cg):
            def take(a):
                return jnp.concatenate(
                    [tin[a, pl.ds(cg * 4 + cc, 64, stride=W), :] for cc in range(4)], axis=0
                ).astype(BF16)

            qb, kb, vb, gb = take(0), take(1), take(2), take(3)
            s = jnp.where(column, nt(kb, qb), NEG)
            probs, ds = softmax_parts([nt(pkh, qb), s], [nt(pvh, gb), nt(vb, gb)])
            p_pre, p = probs[0].astype(BF16), probs[1].astype(BF16)
            ds_pre, dd = ds[0].astype(BF16), ds[1].astype(BF16)
            dq = jnp.transpose(tn(pkh, ds_pre) + tn(kb, dd)) * SCALE
            dk = nn(dd, qb) * SCALE
            dv = nn(p, gb)
            accp[0, 2 * h + 1] += nn(ds_pre, qb)
            accp[1, 2 * h + 1] += nn(p_pre, gb)
            for a, val in enumerate((dq, dk, dv)):
                for cc in range(4):
                    tout[a, pl.ds(cg * 4 + cc, 64, stride=W), :] = val[cc * 64 : cc * 64 + 64]

        for a in range(3):
            @pl.loop(0, N)
            def _(b):
                st2[h, b, a] = tout[a, pl.ds(b * 64, 64)].astype(BF16).reshape(2, W, DH)

    sent2 = [[], []]
    own = []

    def send_back(h):
        own.append(pltpu.make_async_copy(st2.at[h, me], rc2.at[h, me], osem.at[h]))
        own[-1].start()
        for j, to in enumerate(ids):
            sent2[h].append(
                remote(st2.at[h, to], rc2.at[h, me], ssem2.at[h, j], rsem2.at[h, j], to)
            )

    for h in range(2):
        mine = pltpu.make_async_copy(st.at[h, me], rc.at[h, me], osem.at[2 + h])
        mine.start()
        mine.wait()
        for c in sent[h]:
            c.wait_recv()
        odd_head(h)
        if h == 0:
            send_back(0)

    for a in range(2):
        for hh in range(4):
            part = accp[a, hh] * SCALE if a == 0 else accp[a, hh]
            at = (a * 4 + hh) * 4
            pgs[at : at + 4] = part.astype(BF16).reshape(4, 16, DH)
    scat = []
    for j, to in enumerate(ids):
        scat.append(remote(pgs.at[to], prs.at[me], pss.at[j], prr.at[j], to))
    send_back(1)
    prs[me] = pgs[me]
    for c in scat:
        c.wait_recv()
    tot = prs[0].astype(F32)
    for j in range(1, N):
        tot = tot + prs[j].astype(F32)
    pag[me] = tot
    gath = []
    for j, to in enumerate(ids):
        gath.append(remote(pag.at[me], pag.at[me], pas.at[j], par.at[j], to))

    n_out = 4
    outs = []

    def put(src, dst, at):
        c = pltpu.make_async_copy(src, dst, osem.at[at])
        c.start()
        outs.append(c)

    for h in range(2):
        back[h].wait_recv()
        for a, (acc, o) in enumerate(((acck, okk), (accv, ov))):
            f = SCALE if a == 0 else 1.0
            o[h, 0] = (acc[h, C : 2 * C] * f).astype(BF16).reshape(N, W, DH)
            o[h, 1] = (acc[h, 2 * C :] * f + hr[h, a].astype(F32)).astype(BF16).reshape(N, W, DH)
        for o, dst in ((oq, dq_o), (okk, dk_o), (ov, dv_o)):
            put(o.at[h], dst.at[:, :, :, lane(2 * h)], n_out)
            n_out += 1

    for h in range(2):
        own[h].wait()
        for c in sent2[h]:
            c.wait_recv()
        for a, dst in enumerate((dq_o, dk_o, dv_o)):
            for r in range(2):
                put(rc2.at[h, :, a, r], dst.at[r, :, :, lane(2 * h + 1)], n_out)
                n_out += 1

    for c in gath:
        c.wait_recv()
    for a, dst in enumerate((pkg_o, pvg_o)):
        for hh in range(4):
            at = (a * 4 + hh) * 4
            dst[:, hh * DH : (hh + 1) * DH] = pag[at : at + 4].reshape(NPRE, DH)

    for c in outs:
        c.wait()
    for c in halo + sent[0] + sent[1] + back + sent2[0] + sent2[1] + scat + gath:
        c.wait_send()


def body(queries, key_field, value_field, out_grad, prefix_keys, prefix_values):
    grid = (2, N, W, 4 * DH)
    anyspace = pl.BlockSpec(memory_space=pl.ANY)
    vm = pl.BlockSpec(memory_space=pltpu.VMEM)
    dma = pltpu.SemaphoreType.DMA
    big = jax.ShapeDtypeStruct(grid, BF16)
    pre = jax.ShapeDtypeStruct((NPRE, 4 * DH), F32)
    dq, dk, dv, pkg, pvg = pl.pallas_call(
        kernel,
        name="strided_backward",
        out_shape=(big, big, big, pre, pre),
        in_specs=[anyspace] * 4 + [vm] * 2,
        out_specs=[anyspace] * 3 + [vm] * 2,
        scratch_shapes=[
            pltpu.VMEM((2, N, 4, 2, W, DH), BF16),
            pltpu.VMEM((2, N, 4, 2, W, DH), BF16),
            pltpu.VMEM((2, 2, N, W, DH), BF16),
            pltpu.VMEM((2, 2, N, W, DH), BF16),
            pltpu.VMEM((2, 3, N, W, DH), BF16),
            pltpu.VMEM((2, 3, N, W, DH), BF16),
            pltpu.VMEM((4, NPRE, DH), BF16),
            pltpu.VMEM((4, NPRE, DH), BF16),
            pltpu.VMEM((2, 3 * C, DH), F32),
            pltpu.VMEM((2, 3 * C, DH), F32),
            pltpu.VMEM((2, 4, NPRE, DH), F32),
            pltpu.VMEM((2, 2, N, W, DH), BF16),
            pltpu.VMEM((2, 2, N, W, DH), BF16),
            pltpu.VMEM((2, 2, N, W, DH), BF16),
            pltpu.VMEM((2, 2, C, DH), BF16),
            pltpu.VMEM((2, 2, C, DH), BF16),
            pltpu.VMEM((4, 2 * C, DH), F32),
            pltpu.VMEM((3, 2 * C, DH), F32),
            pltpu.VMEM((2, N, 3, 2, W, DH), BF16),
            pltpu.VMEM((2, N, 3, 2, W, DH), BF16),
            pltpu.VMEM((N, 16, DH), BF16),
            pltpu.VMEM((N, 16, DH), BF16),
            pltpu.VMEM((N, 16, DH), F32),
            dma((32,)),
            dma((2, N - 1)), dma((2, N - 1)),
            dma((4,)), dma((4,)), dma((2,)), dma((2,)),
            dma((2, N - 1)), dma((2, N - 1)),
            dma((N - 1,)), dma((N - 1,)), dma((N - 1,)), dma((N - 1,)),
            dma((22,)),
        ],
        compiler_params=pltpu.CompilerParams(
            collective_id=0, has_side_effects=True, vmem_limit_bytes=60 << 20
        ),
    )(
        *[a.reshape(grid) for a in (queries, key_field, value_field, out_grad)],
        prefix_keys,
        prefix_values,
    )
    flat = (2 * C, 4 * DH)
    return dq.reshape(flat), dk.reshape(flat), dv.reshape(flat), pkg, pvg


def solution(mesh):
    split = P("seq", "head")
    shared = P(None, "head")
    return jax.shard_map(
        body,
        mesh=mesh,
        in_specs=(split, split, split, split, shared, shared),
        out_specs=(split, split, split, shared, shared),
        check_vma=False,
    )
```

```python
import math

import jax
import jax.numpy as jnp
from jax import lax
from jax.experimental import pallas as pl
from jax.experimental.pallas import tpu as pltpu
from jax.sharding import PartitionSpec as P

DH = 128
C = 1024
NPRE = 64
N = 32
W = C // N
QB = 256
KB = QB + C
SCALE = 1.0 / math.sqrt(DH)
LOG2E = SCALE * math.log2(math.e)
NEG = -1e30
MESH = pl.DeviceIdType.MESH
F32 = jnp.float32
BF16 = jnp.bfloat16

ORDER = [
    (1, 2, 3), (0, 0, 1), (1, 3, 2), (0, 1, 0), (1, 2, 1), (0, 0, 3), (1, 2, 2), (0, 3, 0),
    (1, 1, 2), (0, 2, 0), (1, 0, 2), (0, 1, 1), (1, 3, 3), (0, 0, 2), (1, 2, 0), (0, 3, 3),
    (1, 1, 1), (1, 0, 0), (0, 2, 2), (0, 3, 1), (1, 1, 3), (0, 1, 2), (1, 3, 0), (0, 1, 3),
    (1, 3, 1), (0, 2, 3), (1, 0, 1), (1, 0, 3), (0, 2, 1), (1, 1, 0), (0, 3, 2),
]


def nt(a, b):
    return lax.dot_general(a, b, (((1,), (1,)), ((), ())), preferred_element_type=F32)


def nn(a, b):
    return lax.dot_general(a, b, (((1,), (0,)), ((), ())), preferred_element_type=F32)


def tn(a, b):
    return lax.dot_general(a, b, (((0,), (0,)), ((), ())), preferred_element_type=F32)


def rows(x):
    return x.reshape(x.shape[-3] * W, DH) if x.ndim == 3 else x.reshape(-1, DH)


def softmax_parts(parts, dparts):
    top = parts[0].max(axis=0, keepdims=True)
    for s in parts[1:]:
        top = jnp.maximum(top, s.max(axis=0, keepdims=True))
    exps = [jnp.exp2((s - top) * LOG2E) for s in parts]
    total = sum(e.sum(axis=0, keepdims=True) for e in exps)
    mixed = sum((e * d).sum(axis=0, keepdims=True) for e, d in zip(exps, dparts))
    inv = 1.0 / total
    delta = mixed * inv
    lse = top * LOG2E + jnp.log2(total)
    probs = [e * inv for e in exps]
    ds = [p * (d - delta) for p, d in zip(probs, dparts)]
    return probs, ds, lse, delta


def kernel(
    q, k, v, g, pk, pv, ev, rc2, pag,
    st, rc, qe, ge, kx, vx, qn, gn, pks, pvs, acck, accv, accp, oe, stat, statn,
    tin, tout, st2, pgs, prs, psum,
    lsem, ssem, rsem, hssem, hrsem, h2s, h2r, ssem2, rsem2, pss, prr, pas, par, osem,
):
    me = lax.axis_index("seq")
    z, x, y = me // 16, (me // 4) % 4, me % 4
    ids = [((z + dz) % 2) * 16 + ((x + dx) % 4) * 4 + (y + dy) % 4 for dz, dx, dy in ORDER]
    nxt = (me + 1) % N
    prv = (me + N - 1) % N

    def lane(hh):
        return pl.ds(hh * DH, DH)

    stage = []
    n = 0
    for h in range(2):
        for a, ref in enumerate((q, k, v, g)):
            for r in range(2):
                c = pltpu.make_async_copy(
                    ref.at[r, :, :, lane(2 * h + 1)], st.at[h, :, a, r], lsem.at[n]
                )
                c.start()
                stage.append(c)
                n += 1
    even = []
    for h in range(2):
        for ref, dst in ((k, kx), (v, vx), (q, qe), (g, ge)):
            off = 1 if ref is k or ref is v else 0
            for r in range(2):
                c = pltpu.make_async_copy(
                    ref.at[r, :, :, lane(2 * h)], dst.at[h, r + off], lsem.at[n]
                )
                c.start()
                even.append(c)
                n += 1

    bar = pltpu.get_barrier_semaphore()
    for i in ids:
        pl.semaphore_signal(bar, inc=1, device_id={"seq": i}, device_id_type=MESH)
    for hh in range(4):
        pks[hh] = pk[:, hh * DH : (hh + 1) * DH]
        pvs[hh] = pv[:, hh * DH : (hh + 1) * DH]
    acck[...] = jnp.zeros_like(acck)
    accv[...] = jnp.zeros_like(accv)
    accp[...] = jnp.zeros_like(accp)
    pl.semaphore_wait(bar, N - 1)

    def remote(src, dst, s, r, to):
        c = pltpu.make_async_remote_copy(
            src_ref=src, dst_ref=dst, send_sem=s, recv_sem=r,
            device_id={"seq": to}, device_id_type=MESH,
        )
        c.start()
        return c

    for c in even:
        c.wait()
    halo = []

    def send_halo(n):
        m = n // 2
        h, a, p = m // 8, (m // 4) % 2, m % 4
        part = pl.ds(p * 8, 8)
        if n % 2 == 0:
            ref = (kx, vx)[a]
            src, dst, to = ref.at[h, 2, part], ref.at[h, 0, part], nxt
        else:
            src, dst, to = (qe, ge)[a].at[h, 0, part], (qn, gn)[a].at[h, part], prv
        halo.append(remote(src, dst, hssem.at[n], hrsem.at[n], to))

    sent = [[], []]
    for h in range(2):
        for c in stage[8 * h : 8 * h + 8]:
            c.wait()
        for j, to in enumerate(ids):
            if h == 0:
                send_halo(j)
            sent[h].append(
                remote(st.at[h, to], rc.at[h, me], ssem.at[h, j], rsem.at[h, j], to)
            )
        if h == 0:
            send_halo(31)

    key_at = lax.broadcasted_iota(jnp.int32, (QB, QB), 0)
    query_at = lax.broadcasted_iota(jnp.int32, (QB, QB), 1)
    causal = key_at <= query_at

    def even_block(h, i):
        qb = rows(qe[h, i // 4, pl.ds((i % 4) * 8, 8)])
        gb = rows(ge[h, i // 4, pl.ds((i % 4) * 8, 8)])

        def window(ref, j):
            at = i + j
            return rows(ref[h, at // 4, pl.ds((at % 4) * 8, 8)])

        ks = [window(kx, j) for j in range(5)]
        vs = [window(vx, j) for j in range(5)]
        pkh, pvh = pks[2 * h], pvs[2 * h]
        s = [nt(kk, qb) for kk in ks]
        for j in range(4):
            s[j] = s[j] + jnp.where((me == 0) & (i + j < 4), NEG, 0.0).astype(F32)
        d = [nt(vv, gb) for vv in vs]
        s0 = jnp.where(causal, s[4], s[0])
        d0 = jnp.where(causal, d[4], d[0])
        probs, ds, lse, delta = softmax_parts(
            [nt(pkh, qb), s0, s[1], s[2], s[3]], [nt(pvh, gb), d0, d[1], d[2], d[3]]
        )

        def spread(parts):
            pre, edge, mid = parts[0], parts[1], parts[2:]
            zero = jnp.zeros_like(edge)
            out = [jnp.where(causal, zero, edge), *mid, jnp.where(causal, edge, zero)]
            return pre.astype(BF16), [o.astype(BF16) for o in out]

        p_pre, p = spread(probs)
        ds_pre, dd = spread(ds)
        dq = tn(pkh, ds_pre)
        for j in range(5):
            at = pl.ds((i + j) * QB, QB)
            accv[h, at] += nn(p[j], gb)
            acck[h, at] += nn(dd[j], qb)
            dq = dq + tn(ks[j], dd[j])
        accp[0, 2 * h] += nn(ds_pre, qb)
        accp[1, 2 * h] += nn(p_pre, gb)
        oe[h, 0, i // 4, pl.ds((i % 4) * 8, 8)] = (
            (jnp.transpose(dq) * SCALE).astype(BF16).reshape(QB // W, W, DH)
        )
        return lse, delta

    @pl.loop(0, 8)
    def _(step):
        even_block(step // 4, step % 4 + 4)

    def first_row():
        for c in halo:
            c.wait_recv()

        @pl.loop(0, 8)
        def _(step):
            lse, delta = even_block(step // 4, step % 4)
            stat[0, pl.ds(step, 1)] = lse
            stat[1, pl.ds(step, 1)] = delta

        return remote(stat, statn, h2s.at[0], h2r.at[0], prv)

    def next_row():
        off = jnp.where(me == N - 1, -NEG, 0.0).astype(F32)

        @pl.loop(0, 4)
        def _(j):
            @pl.loop(0, j + 1)
            def _(i):
                for h in range(2):
                    kb = rows(kx[h, 2, pl.ds(j * 8, 8)])
                    vb = rows(vx[h, 2, pl.ds(j * 8, 8)])
                    qb = rows(qn[h, pl.ds(i * 8, 8)])
                    gb = rows(gn[h, pl.ds(i * 8, 8)])
                    lse = statn[0, pl.ds(h * 4 + i, 1)] + off
                    delta = statn[1, pl.ds(h * 4 + i, 1)]
                    s = jnp.where(causal & (i == j), NEG, nt(kb, qb))
                    p = jnp.exp2(s * LOG2E - lse)
                    ds = p * (nt(vb, gb) - delta)
                    at = pl.ds(2 * C + j * QB, QB)
                    accv[h, at] += nn(p.astype(BF16), gb)
                    acck[h, at] += nn(ds.astype(BF16), qb)

    key_col = key_at // 64
    query_col = query_at // 64
    column = (key_col == query_col) & (key_at % 64 <= query_at % 64)

    def odd_head(h):
        @pl.loop(0, N, unroll=2)
        def _(b):
            for a in range(4):
                tin[a, pl.ds(b * 64, 64)] = rows(rc[h, b, a]).astype(F32)

        pkh, pvh = pks[2 * h + 1], pvs[2 * h + 1]

        @pl.loop(0, W // 4, unroll=2)
        def _(cg):
            def take(a):
                return jnp.concatenate(
                    [tin[a, pl.ds(cg * 4 + cc, 64, stride=W), :] for cc in range(4)], axis=0
                ).astype(BF16)

            qb, kb, vb, gb = take(0), take(1), take(2), take(3)
            s = jnp.where(column, nt(kb, qb), NEG)
            probs, ds, _, _ = softmax_parts([nt(pkh, qb), s], [nt(pvh, gb), nt(vb, gb)])
            p_pre, p = probs[0].astype(BF16), probs[1].astype(BF16)
            ds_pre, dd = ds[0].astype(BF16), ds[1].astype(BF16)
            dq = jnp.transpose(tn(pkh, ds_pre) + tn(kb, dd)) * SCALE
            dk = nn(dd, qb) * SCALE
            dv = nn(p, gb)
            accp[0, 2 * h + 1] += nn(ds_pre, qb)
            accp[1, 2 * h + 1] += nn(p_pre, gb)
            for a, val in enumerate((dq, dk, dv)):
                for cc in range(4):
                    tout[a, pl.ds(cg * 4 + cc, 64, stride=W), :] = val[cc * 64 : cc * 64 + 64]

        @pl.loop(0, N, unroll=2)
        def _(b):
            for a in range(3):
                st2[h, b, a] = tout[a, pl.ds(b * 64, 64)].astype(BF16).reshape(2, W, DH)

    sent2 = [[], []]
    outs = []

    def put(src, dst):
        c = pltpu.make_async_copy(src, dst, osem.at[len(outs)])
        c.start()
        outs.append(c)

    def send_back(h, lo, hi):
        for j in range(lo, hi):
            sent2[h].append(
                remote(st2.at[h, ids[j]], rc2.at[h, me], ssem2.at[h, j], rsem2.at[h, j], ids[j])
            )

    for h in range(2):
        mine = pltpu.make_async_copy(st.at[h, me], rc.at[h, me], lsem.at[32 + h])
        mine.start()
        mine.wait()
        for c in sent[h]:
            c.wait_recv()
        odd_head(h)
        put(st2.at[h, me], rc2.at[h, me])
        if h == 0:
            send_back(0, 0, N - 1)
            stats = first_row()

    for a in range(2):
        for hh in range(4):
            part = accp[a, hh] * SCALE if a == 0 else accp[a, hh]
            at = (a * 4 + hh) * 4
            pgs[at : at + 4] = part.astype(BF16).reshape(4, 16, DH)
    scat = []
    for j, to in enumerate(ids):
        scat.append(remote(pgs.at[to], prs.at[me], pss.at[j], prr.at[j], to))
    send_back(1, 0, 4)
    prs[me] = pgs[me]
    for c in scat:
        c.wait_recv()
    tot = prs[0].astype(F32)
    for j in range(1, N):
        tot = tot + prs[j].astype(F32)
    psum[...] = tot.astype(BF16)
    put(psum, pag.at[me])
    gath = []
    for j, to in enumerate(ids):
        gath.append(remote(psum, pag.at[me], pas.at[j], par.at[j], to))
    send_back(1, 4, N - 1)

    stats.wait_recv()
    next_row()
    for h in range(2):
        for a, acc in ((1, acck), (2, accv)):
            for r in range(2):
                part = acc[h, (1 + r) * C : (2 + r) * C]
                part = part * SCALE if a == 1 else part
                oe[h, a, r] = part.astype(BF16).reshape(N, W, DH)
        put(oe.at[h], ev.at[h])

    for h in range(2):
        for c in sent2[h]:
            c.wait_recv()
    for c in gath:
        c.wait_recv()
    for c in outs:
        c.wait()
    for c in halo + sent[0] + sent[1] + [stats] + sent2[0] + sent2[1] + scat + gath:
        c.wait_send()


def merge(ev, od, pag, dq, dk, dv, pkg, pvg):
    for a, out in enumerate((dq, dk, dv)):
        for h in range(2):
            out[:, 2 * h * DH : (2 * h + 1) * DH] = ev[h, a, 0].reshape(-1, DH)
            out[:, (2 * h + 1) * DH : (2 * h + 2) * DH] = od[h, :, a, 0].reshape(-1, DH)
    for a, out in enumerate((pkg, pvg)):
        for hh in range(4):
            at = (a * 4 + hh) * 4
            out[:, hh * DH : (hh + 1) * DH] = pag[at : at + 4].reshape(NPRE, DH).astype(F32)


def body(queries, key_field, value_field, out_grad, prefix_keys, prefix_values):
    grid = (2, N, W, 4 * DH)
    anyspace = pl.BlockSpec(memory_space=pl.ANY)
    vm = pl.BlockSpec(memory_space=pltpu.VMEM)
    dma = pltpu.SemaphoreType.DMA
    ev, od, pag = pl.pallas_call(
        kernel,
        name="strided_backward",
        out_shape=(
            jax.ShapeDtypeStruct((2, 3, 2, N, W, DH), BF16),
            jax.ShapeDtypeStruct((2, N, 3, 2, W, DH), BF16),
            jax.ShapeDtypeStruct((N, 16, DH), BF16),
        ),
        in_specs=[anyspace] * 4 + [vm] * 2,
        out_specs=[anyspace] * 3,
        scratch_shapes=[
            pltpu.VMEM((2, N, 4, 2, W, DH), BF16),
            pltpu.VMEM((2, N, 4, 2, W, DH), BF16),
            pltpu.VMEM((2, 2, N, W, DH), BF16),
            pltpu.VMEM((2, 2, N, W, DH), BF16),
            pltpu.VMEM((2, 3, N, W, DH), BF16),
            pltpu.VMEM((2, 3, N, W, DH), BF16),
            pltpu.VMEM((2, N, W, DH), BF16),
            pltpu.VMEM((2, N, W, DH), BF16),
            pltpu.VMEM((4, NPRE, DH), BF16),
            pltpu.VMEM((4, NPRE, DH), BF16),
            pltpu.VMEM((2, 3 * C, DH), F32),
            pltpu.VMEM((2, 3 * C, DH), F32),
            pltpu.VMEM((2, 4, NPRE, DH), F32),
            pltpu.VMEM((2, 3, 2, N, W, DH), BF16),
            pltpu.VMEM((2, 8, QB), F32),
            pltpu.VMEM((2, 8, QB), F32),
            pltpu.VMEM((4, 2 * C, DH), F32),
            pltpu.VMEM((3, 2 * C, DH), F32),
            pltpu.VMEM((2, N, 3, 2, W, DH), BF16),
            pltpu.VMEM((N, 16, DH), BF16),
            pltpu.VMEM((N, 16, DH), BF16),
            pltpu.VMEM((16, DH), BF16),
            dma((34,)),
            dma((2, N - 1)), dma((2, N - 1)),
            dma((32,)), dma((32,)), dma((1,)), dma((1,)),
            dma((2, N - 1)), dma((2, N - 1)),
            dma((N - 1,)), dma((N - 1,)), dma((N - 1,)), dma((N - 1,)),
            dma((5,)),
        ],
        compiler_params=pltpu.CompilerParams(
            collective_id=0, has_side_effects=True, vmem_limit_bytes=60 << 20
        ),
    )(
        *[a.reshape(grid) for a in (queries, key_field, value_field, out_grad)],
        prefix_keys,
        prefix_values,
    )
    steps = 8
    wide = pl.BlockSpec((2 * C // steps, 4 * DH), lambda p: (p, 0))
    pre = pl.BlockSpec((NPRE, 4 * DH), lambda p: (0, 0))
    big = jax.ShapeDtypeStruct((2 * C, 4 * DH), BF16)
    small = jax.ShapeDtypeStruct((NPRE, 4 * DH), F32)
    blk = 2 * N // steps
    half = steps // 2
    return pl.pallas_call(
        merge,
        name="merge_heads",
        grid=(steps,),
        out_shape=(big, big, big, small, small),
        in_specs=[
            pl.BlockSpec((2, 3, 1, blk, W, DH), lambda p: (0, 0, p // half, p % half, 0, 0)),
            pl.BlockSpec((2, blk, 3, 1, W, DH), lambda p: (0, p % half, 0, p // half, 0, 0)),
            pl.BlockSpec((N, 16, DH), lambda p: (0, 0, 0)),
        ],
        out_specs=[wide] * 3 + [pre] * 2,
        compiler_params=pltpu.CompilerParams(vmem_limit_bytes=60 << 20),
    )(ev, od, pag)


def solution(mesh):
    split = P("seq", "head")
    shared = P(None, "head")
    return jax.shard_map(
        body,
        mesh=mesh,
        in_specs=(split, split, split, split, shared, shared),
        out_specs=(split, split, split, shared, shared),
        check_vma=False,
    )
```

```python
import math

import jax
import jax.numpy as jnp
from jax import lax
from jax.experimental import pallas as pl
from jax.experimental.pallas import tpu as pltpu
from jax.sharding import PartitionSpec as P

DH = 128
C = 1024
NPRE = 64
N = 32
W = C // N
QB = 256
KB = QB + C
SCALE = 1.0 / math.sqrt(DH)
LOG2E = SCALE * math.log2(math.e)
NEG = -1e30
MESH = pl.DeviceIdType.MESH
F32 = jnp.float32
BF16 = jnp.bfloat16

ORDER = [
    (1, 2, 3), (0, 0, 1), (1, 3, 2), (0, 1, 0), (1, 2, 1), (0, 0, 3), (1, 2, 2), (0, 3, 0),
    (1, 1, 2), (0, 2, 0), (1, 0, 2), (0, 1, 1), (1, 3, 3), (0, 0, 2), (1, 2, 0), (0, 3, 3),
    (1, 1, 1), (1, 0, 0), (0, 2, 2), (0, 3, 1), (1, 1, 3), (0, 1, 2), (1, 3, 0), (0, 1, 3),
    (1, 3, 1), (0, 2, 3), (1, 0, 1), (1, 0, 3), (0, 2, 1), (1, 1, 0), (0, 3, 2),
]


def nt(a, b):
    return lax.dot_general(a, b, (((1,), (1,)), ((), ())), preferred_element_type=F32)


def nn(a, b):
    return lax.dot_general(a, b, (((1,), (0,)), ((), ())), preferred_element_type=F32)


def tn(a, b):
    return lax.dot_general(a, b, (((0,), (0,)), ((), ())), preferred_element_type=F32)


def rows(x):
    return x.reshape(x.shape[-3] * W, DH) if x.ndim == 3 else x.reshape(-1, DH)


def softmax_parts(parts, dparts):
    top = parts[0].max(axis=0, keepdims=True)
    for s in parts[1:]:
        top = jnp.maximum(top, s.max(axis=0, keepdims=True))
    exps = [jnp.exp2((s - top) * LOG2E) for s in parts]
    total = sum(e.sum(axis=0, keepdims=True) for e in exps)
    mixed = sum((e * d).sum(axis=0, keepdims=True) for e, d in zip(exps, dparts))
    inv = 1.0 / total
    delta = mixed * inv
    lse = top * LOG2E + jnp.log2(total)
    probs = [e * inv for e in exps]
    ds = [p * (d - delta) for p, d in zip(probs, dparts)]
    return probs, ds, lse, delta


def kernel(
    q, k, v, g, pk, pv, ev, rc2, pag,
    st, rc, qe, ge, kx, vx, qn, gn, pks, pvs, acck, accv, accp, oe, stat, statn,
    tin, tout, st2, pgs, prs, psum,
    lsem, ssem, rsem, hssem, hrsem, h2s, h2r, ssem2, rsem2, pss, prr, pas, par, osem,
):
    me = lax.axis_index("seq")
    z, x, y = me // 16, (me // 4) % 4, me % 4
    ids = [((z + dz) % 2) * 16 + ((x + dx) % 4) * 4 + (y + dy) % 4 for dz, dx, dy in ORDER]
    nxt = (me + 1) % N
    prv = (me + N - 1) % N

    def lane(hh):
        return pl.ds(hh * DH, DH)

    stage = []
    n = 0
    for h in range(2):
        for a, ref in enumerate((q, k, v, g)):
            for r in range(2):
                c = pltpu.make_async_copy(
                    ref.at[r, :, :, lane(2 * h + 1)], st.at[h, :, a, r], lsem.at[n]
                )
                c.start()
                stage.append(c)
                n += 1
    even = []
    for h in range(2):
        for ref, dst in ((k, kx), (v, vx), (q, qe), (g, ge)):
            off = 1 if ref is k or ref is v else 0
            for r in range(2):
                c = pltpu.make_async_copy(
                    ref.at[r, :, :, lane(2 * h)], dst.at[h, r + off], lsem.at[n]
                )
                c.start()
                even.append(c)
                n += 1

    bar = pltpu.get_barrier_semaphore()
    for i in ids:
        pl.semaphore_signal(bar, inc=1, device_id={"seq": i}, device_id_type=MESH)
    for hh in range(4):
        pks[hh] = pk[:, hh * DH : (hh + 1) * DH]
        pvs[hh] = pv[:, hh * DH : (hh + 1) * DH]
    acck[...] = jnp.zeros_like(acck)
    accv[...] = jnp.zeros_like(accv)
    accp[...] = jnp.zeros_like(accp)
    pl.semaphore_wait(bar, N - 1)

    def remote(src, dst, s, r, to):
        c = pltpu.make_async_remote_copy(
            src_ref=src, dst_ref=dst, send_sem=s, recv_sem=r,
            device_id={"seq": to}, device_id_type=MESH,
        )
        c.start()
        return c

    for c in even:
        c.wait()
    halo = []

    def send_halo(n):
        h, a = n // 4, n // 2 % 2
        if n % 2 == 0:
            ref = (kx, vx)[a]
            src, dst, to = ref.at[h, 2], ref.at[h, 0], nxt
        else:
            src, dst, to = (qe, ge)[a].at[h, 0], (qn, gn)[a].at[h], prv
        halo.append(remote(src, dst, hssem.at[n], hrsem.at[n], to))

    sent = [[], []]
    sent2 = [[], []]

    def send_in(h, j):
        sent[h].append(
            remote(st.at[h, ids[j]], rc.at[h, me], ssem.at[h, j], rsem.at[h, j], ids[j])
        )

    def send_back(h, j):
        sent2[h].append(
            remote(st2.at[h, ids[j]], rc2.at[h, me], ssem2.at[h, j], rsem2.at[h, j], ids[j])
        )

    for n in range(8):
        send_halo(n)

    key_at = lax.broadcasted_iota(jnp.int32, (QB, QB), 0)
    query_at = lax.broadcasted_iota(jnp.int32, (QB, QB), 1)
    causal = key_at <= query_at

    def even_block(h, i):
        qb = rows(qe[h, i // 4, pl.ds((i % 4) * 8, 8)])
        gb = rows(ge[h, i // 4, pl.ds((i % 4) * 8, 8)])

        def window(ref, j):
            at = i + j
            return rows(ref[h, at // 4, pl.ds((at % 4) * 8, 8)])

        ks = [window(kx, j) for j in range(5)]
        vs = [window(vx, j) for j in range(5)]
        pkh, pvh = pks[2 * h], pvs[2 * h]
        s = [nt(kk, qb) for kk in ks]
        for j in range(4):
            s[j] = s[j] + jnp.where((me == 0) & (i + j < 4), NEG, 0.0).astype(F32)
        d = [nt(vv, gb) for vv in vs]
        s0 = jnp.where(causal, s[4], s[0])
        d0 = jnp.where(causal, d[4], d[0])
        probs, ds, lse, delta = softmax_parts(
            [nt(pkh, qb), s0, s[1], s[2], s[3]], [nt(pvh, gb), d0, d[1], d[2], d[3]]
        )

        def spread(parts):
            pre, edge, mid = parts[0], parts[1], parts[2:]
            zero = jnp.zeros_like(edge)
            out = [jnp.where(causal, zero, edge), *mid, jnp.where(causal, edge, zero)]
            return pre.astype(BF16), [o.astype(BF16) for o in out]

        p_pre, p = spread(probs)
        ds_pre, dd = spread(ds)
        dq = tn(pkh, ds_pre)
        for j in range(5):
            at = pl.ds((i + j) * QB, QB)
            accv[h, at] += nn(p[j], gb)
            acck[h, at] += nn(dd[j], qb)
            dq = dq + tn(ks[j], dd[j])
        accp[0, 2 * h] += nn(ds_pre, qb)
        accp[1, 2 * h] += nn(p_pre, gb)
        oe[h, 0, i // 4, pl.ds((i % 4) * 8, 8)] = (
            (jnp.transpose(dq) * SCALE).astype(BF16).reshape(QB // W, W, DH)
        )
        return lse, delta

    @pl.loop(4, 8)
    def _(i):
        for h in range(2):
            even_block(h, i)

    for c in halo:
        c.wait()
    for h in range(2):
        for c in stage[8 * h : 8 * h + 8]:
            c.wait()
        for j in range(N - 1):
            send_in(h, j)

    def first_row():
        @pl.loop(0, 4)
        def _(i):
            for h in range(2):
                lse, delta = even_block(h, i)
                stat[0, pl.ds(h * 4 + i, 1)] = lse
                stat[1, pl.ds(h * 4 + i, 1)] = delta

        return remote(stat, statn, h2s.at[0], h2r.at[0], prv)

    def next_row():
        off = jnp.where(me == N - 1, -NEG, 0.0).astype(F32)

        @pl.loop(0, 4)
        def _(j):
            @pl.loop(0, j + 1)
            def _(i):
                for h in range(2):
                    kb = rows(kx[h, 2, pl.ds(j * 8, 8)])
                    vb = rows(vx[h, 2, pl.ds(j * 8, 8)])
                    qb = rows(qn[h, pl.ds(i * 8, 8)])
                    gb = rows(gn[h, pl.ds(i * 8, 8)])
                    lse = statn[0, pl.ds(h * 4 + i, 1)] + off
                    delta = statn[1, pl.ds(h * 4 + i, 1)]
                    s = jnp.where(causal & (i == j), NEG, nt(kb, qb))
                    p = jnp.exp2(s * LOG2E - lse)
                    ds = p * (nt(vb, gb) - delta)
                    at = pl.ds(2 * C + j * QB, QB)
                    accv[h, at] += nn(p.astype(BF16), gb)
                    acck[h, at] += nn(ds.astype(BF16), qb)

    stats = first_row()

    key_col = key_at // 64
    query_col = query_at // 64
    column = (key_col == query_col) & (key_at % 64 <= query_at % 64)

    def odd_head(h):
        @pl.loop(0, N, unroll=2)
        def _(b):
            for a in range(4):
                tin[a, pl.ds(b * 64, 64)] = rows(rc[h, b, a]).astype(F32)

        pkh, pvh = pks[2 * h + 1], pvs[2 * h + 1]

        @pl.loop(0, W // 4, unroll=2)
        def _(cg):
            def take(a):
                return jnp.concatenate(
                    [tin[a, pl.ds(cg * 4 + cc, 64, stride=W), :] for cc in range(4)], axis=0
                ).astype(BF16)

            qb, kb, vb, gb = take(0), take(1), take(2), take(3)
            s = jnp.where(column, nt(kb, qb), NEG)
            probs, ds, _, _ = softmax_parts([nt(pkh, qb), s], [nt(pvh, gb), nt(vb, gb)])
            p_pre, p = probs[0].astype(BF16), probs[1].astype(BF16)
            ds_pre, dd = ds[0].astype(BF16), ds[1].astype(BF16)
            dq = jnp.transpose(tn(pkh, ds_pre) + tn(kb, dd)) * SCALE
            dk = nn(dd, qb) * SCALE
            dv = nn(p, gb)
            accp[0, 2 * h + 1] += nn(ds_pre, qb)
            accp[1, 2 * h + 1] += nn(p_pre, gb)
            for a, val in enumerate((dq, dk, dv)):
                for cc in range(4):
                    tout[a, pl.ds(cg * 4 + cc, 64, stride=W), :] = val[cc * 64 : cc * 64 + 64]

        @pl.loop(0, N, unroll=2)
        def _(b):
            for a in range(3):
                st2[h, b, a] = tout[a, pl.ds(b * 64, 64)].astype(BF16).reshape(2, W, DH)

    outs = []

    def put(src, dst):
        c = pltpu.make_async_copy(src, dst, osem.at[len(outs)])
        c.start()
        outs.append(c)

    for h in range(2):
        mine = pltpu.make_async_copy(st.at[h, me], rc.at[h, me], lsem.at[32 + h])
        mine.start()
        mine.wait()
        for c in sent[h]:
            c.wait_recv()
        odd_head(h)
        put(st2.at[h, me], rc2.at[h, me])
        if h == 0:
            for j in range(N - 1):
                send_back(0, j)

    for a in range(2):
        for hh in range(4):
            part = accp[a, hh] * SCALE if a == 0 else accp[a, hh]
            at = (a * 4 + hh) * 4
            pgs[at : at + 4] = part.astype(BF16).reshape(4, 16, DH)
    scat = []
    for j, to in enumerate(ids):
        scat.append(remote(pgs.at[to], prs.at[me], pss.at[j], prr.at[j], to))
    for j in range(4):
        send_back(1, j)
    prs[me] = pgs[me]
    for c in scat:
        c.wait_recv()
    tot = prs[0].astype(F32)
    for j in range(1, N):
        tot = tot + prs[j].astype(F32)
    psum[...] = tot.astype(BF16)
    put(psum, pag.at[me])
    gath = []
    for j, to in enumerate(ids):
        gath.append(remote(psum, pag.at[me], pas.at[j], par.at[j], to))
    for j in range(4, N - 1):
        send_back(1, j)

    stats.wait_recv()
    next_row()
    for h in range(2):
        for a, acc in ((1, acck), (2, accv)):
            for r in range(2):
                part = acc[h, (1 + r) * C : (2 + r) * C]
                part = part * SCALE if a == 1 else part
                oe[h, a, r] = part.astype(BF16).reshape(N, W, DH)
        put(oe.at[h], ev.at[h])

    for h in range(2):
        for c in sent2[h]:
            c.wait_recv()
    for c in gath:
        c.wait_recv()
    for c in outs:
        c.wait()
    for c in sent[0] + sent[1] + [stats] + sent2[0] + sent2[1] + scat + gath:
        c.wait_send()


def merge(ev, od, pag, dq, dk, dv, pkg, pvg):
    for a, out in enumerate((dq, dk, dv)):
        for h in range(2):
            out[:, 2 * h * DH : (2 * h + 1) * DH] = ev[h, a, 0].reshape(-1, DH)
            out[:, (2 * h + 1) * DH : (2 * h + 2) * DH] = od[h, :, a, 0].reshape(-1, DH)
    for a, out in enumerate((pkg, pvg)):
        for hh in range(4):
            at = (a * 4 + hh) * 4
            out[:, hh * DH : (hh + 1) * DH] = pag[at : at + 4].reshape(NPRE, DH).astype(F32)


def body(queries, key_field, value_field, out_grad, prefix_keys, prefix_values):
    grid = (2, N, W, 4 * DH)
    anyspace = pl.BlockSpec(memory_space=pl.ANY)
    vm = pl.BlockSpec(memory_space=pltpu.VMEM)
    dma = pltpu.SemaphoreType.DMA
    ev, od, pag = pl.pallas_call(
        kernel,
        name="strided_backward",
        out_shape=(
            jax.ShapeDtypeStruct((2, 3, 2, N, W, DH), BF16),
            jax.ShapeDtypeStruct((2, N, 3, 2, W, DH), BF16),
            jax.ShapeDtypeStruct((N, 16, DH), BF16),
        ),
        in_specs=[anyspace] * 4 + [vm] * 2,
        out_specs=[anyspace] * 3,
        scratch_shapes=[
            pltpu.VMEM((2, N, 4, 2, W, DH), BF16),
            pltpu.VMEM((2, N, 4, 2, W, DH), BF16),
            pltpu.VMEM((2, 2, N, W, DH), BF16),
            pltpu.VMEM((2, 2, N, W, DH), BF16),
            pltpu.VMEM((2, 3, N, W, DH), BF16),
            pltpu.VMEM((2, 3, N, W, DH), BF16),
            pltpu.VMEM((2, N, W, DH), BF16),
            pltpu.VMEM((2, N, W, DH), BF16),
            pltpu.VMEM((4, NPRE, DH), BF16),
            pltpu.VMEM((4, NPRE, DH), BF16),
            pltpu.VMEM((2, 3 * C, DH), F32),
            pltpu.VMEM((2, 3 * C, DH), F32),
            pltpu.VMEM((2, 4, NPRE, DH), F32),
            pltpu.VMEM((2, 3, 2, N, W, DH), BF16),
            pltpu.VMEM((2, 8, QB), F32),
            pltpu.VMEM((2, 8, QB), F32),
            pltpu.VMEM((4, 2 * C, DH), F32),
            pltpu.VMEM((3, 2 * C, DH), F32),
            pltpu.VMEM((2, N, 3, 2, W, DH), BF16),
            pltpu.VMEM((N, 16, DH), BF16),
            pltpu.VMEM((N, 16, DH), BF16),
            pltpu.VMEM((16, DH), BF16),
            dma((34,)),
            dma((2, N - 1)), dma((2, N - 1)),
            dma((8,)), dma((8,)), dma((1,)), dma((1,)),
            dma((2, N - 1)), dma((2, N - 1)),
            dma((N - 1,)), dma((N - 1,)), dma((N - 1,)), dma((N - 1,)),
            dma((5,)),
        ],
        compiler_params=pltpu.CompilerParams(
            collective_id=0, has_side_effects=True, vmem_limit_bytes=60 << 20
        ),
    )(
        *[a.reshape(grid) for a in (queries, key_field, value_field, out_grad)],
        prefix_keys,
        prefix_values,
    )
    steps = 2
    wide = pl.BlockSpec((2 * C // steps, 4 * DH), lambda p: (p, 0))
    pre = pl.BlockSpec((NPRE, 4 * DH), lambda p: (0, 0))
    big = jax.ShapeDtypeStruct((2 * C, 4 * DH), BF16)
    small = jax.ShapeDtypeStruct((NPRE, 4 * DH), F32)
    blk = 2 * N // steps
    half = steps // 2
    return pl.pallas_call(
        merge,
        name="merge_heads",
        grid=(steps,),
        out_shape=(big, big, big, small, small),
        in_specs=[
            pl.BlockSpec((2, 3, 1, blk, W, DH), lambda p: (0, 0, p // half, p % half, 0, 0)),
            pl.BlockSpec((2, blk, 3, 1, W, DH), lambda p: (0, p % half, 0, p // half, 0, 0)),
            pl.BlockSpec((N, 16, DH), lambda p: (0, 0, 0)),
        ],
        out_specs=[wide] * 3 + [pre] * 2,
        compiler_params=pltpu.CompilerParams(vmem_limit_bytes=60 << 20),
    )(ev, od, pag)


def solution(mesh):
    split = P("seq", "head")
    shared = P(None, "head")
    return jax.shard_map(
        body,
        mesh=mesh,
        in_specs=(split, split, split, split, shared, shared),
        out_specs=(split, split, split, shared, shared),
        check_vma=False,
    )
```

```python
import math

import jax
import jax.numpy as jnp
from jax import lax
from jax.experimental import pallas as pl
from jax.experimental.pallas import tpu as pltpu
from jax.sharding import PartitionSpec as P

DH = 128
C = 1024
NPRE = 64
N = 32
W = C // N
QB = 256
KB = QB + C
SCALE = 1.0 / math.sqrt(DH)
LOG2E = SCALE * math.log2(math.e)
NEG = -1e30
HALF = 16
MESH = pl.DeviceIdType.MESH
F32 = jnp.float32
BF16 = jnp.bfloat16

ORDER = [
    (1, 2, 3), (0, 0, 1), (1, 3, 2), (0, 1, 0), (1, 2, 1), (0, 0, 3), (1, 2, 2), (0, 3, 0),
    (1, 1, 2), (0, 2, 0), (1, 0, 2), (0, 1, 1), (1, 3, 3), (0, 0, 2), (1, 2, 0), (0, 3, 3),
    (1, 1, 1), (1, 0, 0), (0, 2, 2), (0, 3, 1), (1, 1, 3), (0, 1, 2), (1, 3, 0), (0, 1, 3),
    (1, 3, 1), (0, 2, 3), (1, 0, 1), (1, 0, 3), (0, 2, 1), (1, 1, 0), (0, 3, 2),
]


def nt(a, b):
    return lax.dot_general(a, b, (((1,), (1,)), ((), ())), preferred_element_type=F32)


def nn(a, b):
    return lax.dot_general(a, b, (((1,), (0,)), ((), ())), preferred_element_type=F32)


def tn(a, b):
    return lax.dot_general(a, b, (((0,), (0,)), ((), ())), preferred_element_type=F32)


def rows(x):
    return x.reshape(x.shape[-3] * W, DH) if x.ndim == 3 else x.reshape(-1, DH)


def softmax_parts(parts, dparts):
    top = parts[0].max(axis=0, keepdims=True)
    for s in parts[1:]:
        top = jnp.maximum(top, s.max(axis=0, keepdims=True))
    exps = [jnp.exp2((s - top) * LOG2E) for s in parts]
    total = sum(e.sum(axis=0, keepdims=True) for e in exps)
    mixed = sum((e * d).sum(axis=0, keepdims=True) for e, d in zip(exps, dparts))
    inv = 1.0 / total
    delta = mixed * inv
    lse = top * LOG2E + jnp.log2(total)
    probs = [e * inv for e in exps]
    ds = [p * (d - delta) for p, d in zip(probs, dparts)]
    return probs, ds, lse, delta


def kernel(
    q, k, v, g, pk, pv, ev, rc2, pag,
    st, rc, qe, ge, kx, vx, qn, gn, pks, pvs, acck, accv, accp, oe, stat, statn,
    tin, tout, st2, pgs, prs, psum,
    lsem, ssem, rsem, hssem, hrsem, h2s, h2r, ssem2, rsem2, pss, prr, pas, par, osem,
):
    me = lax.axis_index("seq")
    z, x, y = me // 16, (me // 4) % 4, me % 4
    ids = [((z + dz) % 2) * 16 + ((x + dx) % 4) * 4 + (y + dy) % 4 for dz, dx, dy in ORDER]
    nxt = (me + 1) % N
    prv = (me + N - 1) % N

    def lane(hh):
        return pl.ds(hh * DH, DH)

    bar = pltpu.get_barrier_semaphore()
    for i in ids:
        pl.semaphore_signal(bar, inc=1, device_id={"seq": i}, device_id_type=MESH)

    early, even, stage = [], [], []

    def load(src, dst, group):
        n = len(early) + len(even) + len(stage)
        c = pltpu.make_async_copy(src, dst, lsem.at[n])
        c.start()
        group.append(c)

    for group in (early, even):
        for h in range(2):
            for ref, dst, off in ((k, kx, 1), (v, vx, 1), (q, qe, 0), (g, ge, 0)):
                r = off if group is early else 1 - off
                load(ref.at[r, :, :, lane(2 * h)], dst.at[h, r + off], group)
    for h in range(2):
        for a, ref in enumerate((q, k, v, g)):
            for r in range(2):
                load(ref.at[r, :, :, lane(2 * h + 1)], st.at[h, :, a, r], stage)

    for hh in range(4):
        pks[hh] = pk[:, hh * DH : (hh + 1) * DH]
        pvs[hh] = pv[:, hh * DH : (hh + 1) * DH]
    acck[...] = jnp.zeros_like(acck)
    accv[...] = jnp.zeros_like(accv)
    accp[...] = jnp.zeros_like(accp)
    pl.semaphore_wait(bar, N - 1)

    def remote(src, dst, s, r, to):
        c = pltpu.make_async_remote_copy(
            src_ref=src, dst_ref=dst, send_sem=s, recv_sem=r,
            device_id={"seq": to}, device_id_type=MESH,
        )
        c.start()
        return c

    for c in early:
        c.wait()
    halo = []

    def send_halo(n):
        h, a = n // 4, n // 2 % 2
        if n % 2 == 0:
            ref = (kx, vx)[a]
            src, dst, to = ref.at[h, 2], ref.at[h, 0], nxt
        else:
            src, dst, to = (qe, ge)[a].at[h, 0], (qn, gn)[a].at[h], prv
        halo.append(remote(src, dst, hssem.at[n], hrsem.at[n], to))

    sent = [[], []]
    sent2 = [[], []]

    def send_in(h, j):
        sent[h].append(
            remote(st.at[h, ids[j]], rc.at[h, me], ssem.at[h, j], rsem.at[h, j], ids[j])
        )

    def send_back(h, j):
        sent2[h].append(
            remote(st2.at[h, ids[j]], rc2.at[h, me], ssem2.at[h, j], rsem2.at[h, j], ids[j])
        )

    for n in range(8):
        send_halo(n)
    for c in even:
        c.wait()

    key_at = lax.broadcasted_iota(jnp.int32, (QB, QB), 0)
    query_at = lax.broadcasted_iota(jnp.int32, (QB, QB), 1)
    causal = key_at <= query_at

    def even_block(h, i):
        qb = rows(qe[h, i // 4, pl.ds((i % 4) * 8, 8)])
        gb = rows(ge[h, i // 4, pl.ds((i % 4) * 8, 8)])

        def window(ref, j):
            at = i + j
            return rows(ref[h, at // 4, pl.ds((at % 4) * 8, 8)])

        ks = [window(kx, j) for j in range(5)]
        vs = [window(vx, j) for j in range(5)]
        pkh, pvh = pks[2 * h], pvs[2 * h]
        s = [nt(kk, qb) for kk in ks]
        for j in range(4):
            s[j] = s[j] + jnp.where((me == 0) & (i + j < 4), NEG, 0.0).astype(F32)
        d = [nt(vv, gb) for vv in vs]
        s0 = jnp.where(causal, s[4], s[0])
        d0 = jnp.where(causal, d[4], d[0])
        probs, ds, lse, delta = softmax_parts(
            [nt(pkh, qb), s0, s[1], s[2], s[3]], [nt(pvh, gb), d0, d[1], d[2], d[3]]
        )

        def spread(parts):
            pre, edge, mid = parts[0], parts[1], parts[2:]
            zero = jnp.zeros_like(edge)
            out = [jnp.where(causal, zero, edge), *mid, jnp.where(causal, edge, zero)]
            return pre.astype(BF16), [o.astype(BF16) for o in out]

        p_pre, p = spread(probs)
        ds_pre, dd = spread(ds)
        dq = tn(pkh, ds_pre)
        for j in range(5):
            at = pl.ds((i + j) * QB, QB)
            accv[h, at] += nn(p[j], gb)
            acck[h, at] += nn(dd[j], qb)
            dq = dq + tn(ks[j], dd[j])
        accp[0, 2 * h] += nn(ds_pre, qb)
        accp[1, 2 * h] += nn(p_pre, gb)
        oe[h, 0, i // 4, pl.ds((i % 4) * 8, 8)] = (
            (jnp.transpose(dq) * SCALE).astype(BF16).reshape(QB // W, W, DH)
        )
        return lse, delta

    @pl.loop(4, 8)
    def _(i):
        for h in range(2):
            even_block(h, i)

    for c in halo:
        c.wait()
    for c in stage:
        c.wait()
    for j in range(N - 1):
        send_in(0, j)
    for j in range(N - 1):
        send_in(1, j)

    def first_row():
        @pl.loop(0, 4)
        def _(i):
            for h in range(2):
                lse, delta = even_block(h, i)
                stat[0, pl.ds(h * 4 + i, 1)] = lse
                stat[1, pl.ds(h * 4 + i, 1)] = delta

        return remote(stat, statn, h2s.at[0], h2r.at[0], prv)

    def next_row():
        off = jnp.where(me == N - 1, -NEG, 0.0).astype(F32)

        @pl.loop(0, 4)
        def _(j):
            @pl.loop(0, j + 1)
            def _(i):
                for h in range(2):
                    kb = rows(kx[h, 2, pl.ds(j * 8, 8)])
                    vb = rows(vx[h, 2, pl.ds(j * 8, 8)])
                    qb = rows(qn[h, pl.ds(i * 8, 8)])
                    gb = rows(gn[h, pl.ds(i * 8, 8)])
                    lse = statn[0, pl.ds(h * 4 + i, 1)] + off
                    delta = statn[1, pl.ds(h * 4 + i, 1)]
                    s = jnp.where(causal & (i == j), NEG, nt(kb, qb))
                    p = jnp.exp2(s * LOG2E - lse)
                    ds = p * (nt(vb, gb) - delta)
                    at = pl.ds(2 * C + j * QB, QB)
                    accv[h, at] += nn(p.astype(BF16), gb)
                    acck[h, at] += nn(ds.astype(BF16), qb)

    stats = first_row()

    key_col = key_at // 64
    query_col = query_at // 64
    column = (key_col == query_col) & (key_at % 64 <= query_at % 64)

    def odd_head(h):
        @pl.loop(0, N, unroll=2)
        def _(b):
            for a in range(4):
                tin[a, pl.ds(b * 64, 64)] = rows(rc[h, b, a]).astype(F32)

        pkh, pvh = pks[2 * h + 1], pvs[2 * h + 1]

        @pl.loop(0, W // 4, unroll=2)
        def _(cg):
            def take(a):
                return jnp.concatenate(
                    [tin[a, pl.ds(cg * 4 + cc, 64, stride=W), :] for cc in range(4)], axis=0
                ).astype(BF16)

            qb, kb, vb, gb = take(0), take(1), take(2), take(3)
            s = jnp.where(column, nt(kb, qb), NEG)
            probs, ds, _, _ = softmax_parts([nt(pkh, qb), s], [nt(pvh, gb), nt(vb, gb)])
            p_pre, p = probs[0].astype(BF16), probs[1].astype(BF16)
            ds_pre, dd = ds[0].astype(BF16), ds[1].astype(BF16)
            dq = jnp.transpose(tn(pkh, ds_pre) + tn(kb, dd)) * SCALE
            dk = nn(dd, qb) * SCALE
            dv = nn(p, gb)
            accp[0, 2 * h + 1] += nn(ds_pre, qb)
            accp[1, 2 * h + 1] += nn(p_pre, gb)
            for a, val in enumerate((dq, dk, dv)):
                for cc in range(4):
                    tout[a, pl.ds(cg * 4 + cc, 64, stride=W), :] = val[cc * 64 : cc * 64 + 64]

        @pl.loop(0, N, unroll=2)
        def _(b):
            for a in range(3):
                st2[h, b, a] = tout[a, pl.ds(b * 64, 64)].astype(BF16).reshape(2, W, DH)

    outs = []

    def put(src, dst):
        c = pltpu.make_async_copy(src, dst, osem.at[len(outs)])
        c.start()
        outs.append(c)

    def even_out():
        for h in range(2):
            for a, acc in ((1, acck), (2, accv)):
                for r in range(2):
                    part = acc[h, (1 + r) * C : (2 + r) * C]
                    part = part * SCALE if a == 1 else part
                    oe[h, a, r] = part.astype(BF16).reshape(N, W, DH)
            put(oe.at[h], ev.at[h])

    for h in range(2):
        mine = pltpu.make_async_copy(st.at[h, me], rc.at[h, me], lsem.at[32 + h])
        mine.start()
        mine.wait()
        for c in sent[h]:
            c.wait_recv()
        odd_head(h)
        put(st2.at[h, me], rc2.at[h, me])
        if h == 0:
            for j in range(N - 1):
                send_back(0, j)

    for a in range(2):
        for hh in range(4):
            part = accp[a, hh] * SCALE if a == 0 else accp[a, hh]
            at = (a * 4 + hh) * 4
            pgs[at : at + 4] = part.astype(BF16).reshape(4, 16, DH)
    scat = []
    for j, to in enumerate(ids):
        scat.append(remote(pgs.at[to], prs.at[me], pss.at[j], prr.at[j], to))
    for j in range(HALF):
        send_back(1, j)
    prs[me] = pgs[me]
    for c in scat:
        c.wait_recv()
    tot = prs[0].astype(F32)
    for j in range(1, N):
        tot = tot + prs[j].astype(F32)
    psum[...] = tot.astype(BF16)
    put(psum, pag.at[me])
    gath = []
    for j, to in enumerate(ids):
        gath.append(remote(psum, pag.at[me], pas.at[j], par.at[j], to))
    for j in range(HALF, N - 1):
        send_back(1, j)
    stats.wait_recv()
    next_row()
    even_out()

    for h in range(2):
        for c in sent2[h]:
            c.wait_recv()
    for c in gath:
        c.wait_recv()
    for c in outs:
        c.wait()
    for c in sent[0] + sent[1] + [stats] + sent2[0] + sent2[1] + scat + gath:
        c.wait_send()


def merge(ev, od, pag, dq, dk, dv, pkg, pvg):
    for a, out in enumerate((dq, dk, dv)):
        for h in range(2):
            out[:, 2 * h * DH : (2 * h + 1) * DH] = ev[h, a, 0].reshape(-1, DH)
            out[:, (2 * h + 1) * DH : (2 * h + 2) * DH] = od[h, :, a, 0].reshape(-1, DH)
    for a, out in enumerate((pkg, pvg)):
        for hh in range(4):
            at = (a * 4 + hh) * 4
            out[:, hh * DH : (hh + 1) * DH] = pag[at : at + 4].reshape(NPRE, DH).astype(F32)


def body(queries, key_field, value_field, out_grad, prefix_keys, prefix_values):
    grid = (2, N, W, 4 * DH)
    anyspace = pl.BlockSpec(memory_space=pl.ANY)
    vm = pl.BlockSpec(memory_space=pltpu.VMEM)
    dma = pltpu.SemaphoreType.DMA
    ev, od, pag = pl.pallas_call(
        kernel,
        name="strided_backward",
        out_shape=(
            jax.ShapeDtypeStruct((2, 3, 2, N, W, DH), BF16),
            jax.ShapeDtypeStruct((2, N, 3, 2, W, DH), BF16),
            jax.ShapeDtypeStruct((N, 16, DH), BF16),
        ),
        in_specs=[anyspace] * 4 + [vm] * 2,
        out_specs=[anyspace] * 3,
        scratch_shapes=[
            pltpu.VMEM((2, N, 4, 2, W, DH), BF16),
            pltpu.VMEM((2, N, 4, 2, W, DH), BF16),
            pltpu.VMEM((2, 2, N, W, DH), BF16),
            pltpu.VMEM((2, 2, N, W, DH), BF16),
            pltpu.VMEM((2, 3, N, W, DH), BF16),
            pltpu.VMEM((2, 3, N, W, DH), BF16),
            pltpu.VMEM((2, N, W, DH), BF16),
            pltpu.VMEM((2, N, W, DH), BF16),
            pltpu.VMEM((4, NPRE, DH), BF16),
            pltpu.VMEM((4, NPRE, DH), BF16),
            pltpu.VMEM((2, 3 * C, DH), F32),
            pltpu.VMEM((2, 3 * C, DH), F32),
            pltpu.VMEM((2, 4, NPRE, DH), F32),
            pltpu.VMEM((2, 3, 2, N, W, DH), BF16),
            pltpu.VMEM((2, 8, QB), F32),
            pltpu.VMEM((2, 8, QB), F32),
            pltpu.VMEM((4, 2 * C + W, DH), F32),
            pltpu.VMEM((3, 2 * C + W, DH), F32),
            pltpu.VMEM((2, N, 3, 2, W, DH), BF16),
            pltpu.VMEM((N, 16, DH), BF16),
            pltpu.VMEM((N, 16, DH), BF16),
            pltpu.VMEM((16, DH), BF16),
            dma((34,)),
            dma((2, N - 1)), dma((2, N - 1)),
            dma((8,)), dma((8,)), dma((1,)), dma((1,)),
            dma((2, N - 1)), dma((2, N - 1)),
            dma((N - 1,)), dma((N - 1,)), dma((N - 1,)), dma((N - 1,)),
            dma((5,)),
        ],
        compiler_params=pltpu.CompilerParams(
            collective_id=0, has_side_effects=True, vmem_limit_bytes=60 << 20
        ),
    )(
        *[a.reshape(grid) for a in (queries, key_field, value_field, out_grad)],
        prefix_keys,
        prefix_values,
    )
    steps = 2
    wide = pl.BlockSpec((2 * C // steps, 4 * DH), lambda p: (p, 0))
    pre = pl.BlockSpec((NPRE, 4 * DH), lambda p: (0, 0))
    big = jax.ShapeDtypeStruct((2 * C, 4 * DH), BF16)
    small = jax.ShapeDtypeStruct((NPRE, 4 * DH), F32)
    blk = 2 * N // steps
    half = steps // 2
    return pl.pallas_call(
        merge,
        name="merge_heads",
        grid=(steps,),
        out_shape=(big, big, big, small, small),
        in_specs=[
            pl.BlockSpec((2, 3, 1, blk, W, DH), lambda p: (0, 0, p // half, p % half, 0, 0)),
            pl.BlockSpec((2, blk, 3, 1, W, DH), lambda p: (0, p % half, 0, p // half, 0, 0)),
            pl.BlockSpec((N, 16, DH), lambda p: (0, 0, 0)),
        ],
        out_specs=[wide] * 3 + [pre] * 2,
        compiler_params=pltpu.CompilerParams(vmem_limit_bytes=60 << 20),
    )(ev, od, pag)


def solution(mesh):
    split = P("seq", "head")
    shared = P(None, "head")
    return jax.shard_map(
        body,
        mesh=mesh,
        in_specs=(split, split, split, split, shared, shared),
        out_specs=(split, split, split, shared, shared),
        check_vma=False,
    )
```

```python
import math

import jax
import jax.numpy as jnp
from jax import lax
from jax.experimental import pallas as pl
from jax.experimental.pallas import tpu as pltpu
from jax.sharding import PartitionSpec as P

DH = 128
C = 1024
NPRE = 64
N = 32
W = C // N
QB = 256
KB = QB + C
SCALE = 1.0 / math.sqrt(DH)
LOG2E = SCALE * math.log2(math.e)
NEG = -1e30
HALF = 16
MESH = pl.DeviceIdType.MESH
F32 = jnp.float32
BF16 = jnp.bfloat16

ORDER = [
    (1, 2, 3), (0, 0, 1), (1, 3, 2), (0, 1, 0), (1, 2, 1), (0, 0, 3), (1, 2, 2), (0, 3, 0),
    (1, 1, 2), (0, 2, 0), (1, 0, 2), (0, 1, 1), (1, 3, 3), (0, 0, 2), (1, 2, 0), (0, 3, 3),
    (1, 1, 1), (1, 0, 0), (0, 2, 2), (0, 3, 1), (1, 1, 3), (0, 1, 2), (1, 3, 0), (0, 1, 3),
    (1, 3, 1), (0, 2, 3), (1, 0, 1), (1, 0, 3), (0, 2, 1), (1, 1, 0), (0, 3, 2),
]


def nt(a, b):
    return lax.dot_general(a, b, (((1,), (1,)), ((), ())), preferred_element_type=F32)


def nn(a, b):
    return lax.dot_general(a, b, (((1,), (0,)), ((), ())), preferred_element_type=F32)


def tn(a, b):
    return lax.dot_general(a, b, (((0,), (0,)), ((), ())), preferred_element_type=F32)


def rows(x):
    return x.reshape(x.shape[-3] * W, DH) if x.ndim == 3 else x.reshape(-1, DH)


def softmax_parts(parts, dparts):
    top = parts[0].max(axis=0, keepdims=True)
    for s in parts[1:]:
        top = jnp.maximum(top, s.max(axis=0, keepdims=True))
    exps = [jnp.exp2((s - top) * LOG2E) for s in parts]
    total = sum(e.sum(axis=0, keepdims=True) for e in exps)
    mixed = sum((e * d).sum(axis=0, keepdims=True) for e, d in zip(exps, dparts))
    inv = 1.0 / total
    delta = mixed * inv
    lse = top * LOG2E + jnp.log2(total)
    probs = [e * inv for e in exps]
    ds = [p * (d - delta) for p, d in zip(probs, dparts)]
    return probs, ds, lse, delta


def kernel(
    q, k, v, g, pk, pv, ev, rc2, pag,
    st, rc, qe, ge, kx, vx, qn, gn, pks, pvs, acck, accv, accp, oe, stat, statn,
    tin, tout, st2, pgs, prs, psum,
    lsem, ssem, rsem, hssem, hrsem, h2s, h2r, ssem2, rsem2, pss, prr, pas, par, osem,
):
    me = lax.axis_index("seq")
    z, x, y = me // 16, (me // 4) % 4, me % 4
    ids = [((z + dz) % 2) * 16 + ((x + dx) % 4) * 4 + (y + dy) % 4 for dz, dx, dy in ORDER]
    nxt = (me + 1) % N
    prv = (me + N - 1) % N

    def lane(hh):
        return pl.ds(hh * DH, DH)

    bar = pltpu.get_barrier_semaphore()
    for i in ids:
        pl.semaphore_signal(bar, inc=1, device_id={"seq": i}, device_id_type=MESH)

    early, even, stage = [], [], []

    def load(src, dst, group):
        n = len(early) + len(even) + len(stage)
        c = pltpu.make_async_copy(src, dst, lsem.at[n])
        c.start()
        group.append(c)

    for group in (early, even):
        for h in range(2):
            for ref, dst, off in ((k, kx, 1), (v, vx, 1), (q, qe, 0), (g, ge, 0)):
                r = off if group is early else 1 - off
                load(ref.at[r, :, :, lane(2 * h)], dst.at[h, r + off], group)
    for h in range(2):
        for a, ref in enumerate((q, k, v, g)):
            for r in range(2):
                load(ref.at[r, :, :, lane(2 * h + 1)], st.at[h, :, a, r], stage)

    for hh in range(4):
        pks[hh] = pk[:, hh * DH : (hh + 1) * DH]
        pvs[hh] = pv[:, hh * DH : (hh + 1) * DH]
    acck[...] = jnp.zeros_like(acck)
    accv[...] = jnp.zeros_like(accv)
    accp[...] = jnp.zeros_like(accp)
    pl.semaphore_wait(bar, N - 1)

    def remote(src, dst, s, r, to):
        c = pltpu.make_async_remote_copy(
            src_ref=src, dst_ref=dst, send_sem=s, recv_sem=r,
            device_id={"seq": to}, device_id_type=MESH,
        )
        c.start()
        return c

    for c in early:
        c.wait()
    halo = []

    def send_halo(n):
        h, a = n // 4, n // 2 % 2
        if n % 2 == 0:
            ref = (kx, vx)[a]
            src, dst, to = ref.at[h, 2], ref.at[h, 0], nxt
        else:
            src, dst, to = (qe, ge)[a].at[h, 0], (qn, gn)[a].at[h], prv
        halo.append(remote(src, dst, hssem.at[n], hrsem.at[n], to))

    sent = [[], []]
    sent2 = [[], []]

    def send_in(h, j):
        sent[h].append(
            remote(st.at[h, ids[j]], rc.at[h, me], ssem.at[h, j], rsem.at[h, j], ids[j])
        )

    def send_back(h, j):
        sent2[h].append(
            remote(st2.at[h, ids[j]], rc2.at[h, me], ssem2.at[h, j], rsem2.at[h, j], ids[j])
        )

    for n in range(8):
        send_halo(n)
    for c in even:
        c.wait()

    key_at = lax.broadcasted_iota(jnp.int32, (QB, QB), 0)
    query_at = lax.broadcasted_iota(jnp.int32, (QB, QB), 1)
    causal = key_at <= query_at

    def even_block(h, i):
        qb = rows(qe[h, i // 4, pl.ds((i % 4) * 8, 8)])
        gb = rows(ge[h, i // 4, pl.ds((i % 4) * 8, 8)])

        def window(ref, j):
            at = i + j
            return rows(ref[h, at // 4, pl.ds((at % 4) * 8, 8)])

        ks = [window(kx, j) for j in range(5)]
        vs = [window(vx, j) for j in range(5)]
        pkh, pvh = pks[2 * h], pvs[2 * h]
        s = [nt(kk, qb) for kk in ks]
        for j in range(4):
            s[j] = s[j] + jnp.where((me == 0) & (i + j < 4), NEG, 0.0).astype(F32)
        d = [nt(vv, gb) for vv in vs]
        s0 = jnp.where(causal, s[4], s[0])
        d0 = jnp.where(causal, d[4], d[0])
        probs, ds, lse, delta = softmax_parts(
            [nt(pkh, qb), s0, s[1], s[2], s[3]], [nt(pvh, gb), d0, d[1], d[2], d[3]]
        )

        def spread(parts):
            pre, edge, mid = parts[0], parts[1], parts[2:]
            zero = jnp.zeros_like(edge)
            out = [jnp.where(causal, zero, edge), *mid, jnp.where(causal, edge, zero)]
            return pre.astype(BF16), [o.astype(BF16) for o in out]

        p_pre, p = spread(probs)
        ds_pre, dd = spread(ds)
        dq = tn(pkh, ds_pre)
        for j in range(5):
            at = pl.ds((i + j) * QB, QB)
            accv[h, at] += nn(p[j], gb)
            acck[h, at] += nn(dd[j], qb)
            dq = dq + tn(ks[j], dd[j])
        accp[0, 2 * h] += nn(ds_pre, qb)
        accp[1, 2 * h] += nn(p_pre, gb)
        oe[h, 0, i // 4, pl.ds((i % 4) * 8, 8)] = (
            (jnp.transpose(dq) * SCALE).astype(BF16).reshape(QB // W, W, DH)
        )
        return lse, delta

    @pl.loop(4, 8)
    def _(i):
        for h in range(2):
            even_block(h, i)

    for c in halo:
        c.wait()
    for c in stage:
        c.wait()
    for j in range(N - 1):
        send_in(0, j)
    for j in range(N - 1):
        send_in(1, j)

    def first_row():
        @pl.loop(0, 4)
        def _(i):
            for h in range(2):
                lse, delta = even_block(h, i)
                stat[0, pl.ds(h * 4 + i, 1)] = lse
                stat[1, pl.ds(h * 4 + i, 1)] = delta

        return remote(stat, statn, h2s.at[0], h2r.at[0], prv)

    def next_row():
        off = jnp.where(me == N - 1, -NEG, 0.0).astype(F32)

        @pl.loop(0, 4)
        def _(j):
            @pl.loop(0, j + 1)
            def _(i):
                for h in range(2):
                    kb = rows(kx[h, 2, pl.ds(j * 8, 8)])
                    vb = rows(vx[h, 2, pl.ds(j * 8, 8)])
                    qb = rows(qn[h, pl.ds(i * 8, 8)])
                    gb = rows(gn[h, pl.ds(i * 8, 8)])
                    lse = statn[0, pl.ds(h * 4 + i, 1)] + off
                    delta = statn[1, pl.ds(h * 4 + i, 1)]
                    s = jnp.where(causal & (i == j), NEG, nt(kb, qb))
                    p = jnp.exp2(s * LOG2E - lse)
                    ds = p * (nt(vb, gb) - delta)
                    at = pl.ds(2 * C + j * QB, QB)
                    accv[h, at] += nn(p.astype(BF16), gb)
                    acck[h, at] += nn(ds.astype(BF16), qb)

    stats = first_row()

    key_col = key_at // 64
    query_col = query_at // 64
    column = (key_col == query_col) & (key_at % 64 <= query_at % 64)

    def odd_head(h):
        @pl.loop(0, N, unroll=2)
        def _(b):
            for a in range(4):
                tin[a, pl.ds(b * 64, 64)] = rows(rc[h, b, a]).astype(F32)

        pkh, pvh = pks[2 * h + 1], pvs[2 * h + 1]

        @pl.loop(0, W // 4, unroll=2)
        def _(cg):
            def take(a):
                return jnp.concatenate(
                    [tin[a, pl.ds(cg * 4 + cc, 64, stride=W), :] for cc in range(4)], axis=0
                ).astype(BF16)

            qb, kb, vb, gb = take(0), take(1), take(2), take(3)
            s = jnp.where(column, nt(kb, qb), NEG)
            probs, ds, _, _ = softmax_parts([nt(pkh, qb), s], [nt(pvh, gb), nt(vb, gb)])
            p_pre, p = probs[0].astype(BF16), probs[1].astype(BF16)
            ds_pre, dd = ds[0].astype(BF16), ds[1].astype(BF16)
            dq = jnp.transpose(tn(pkh, ds_pre) + tn(kb, dd)) * SCALE
            dk = nn(dd, qb) * SCALE
            dv = nn(p, gb)
            accp[0, 2 * h + 1] += nn(ds_pre, qb)
            accp[1, 2 * h + 1] += nn(p_pre, gb)
            for a, val in enumerate((dq, dk, dv)):
                for cc in range(4):
                    tout[a, pl.ds(cg * 4 + cc, 64, stride=W), :] = val[cc * 64 : cc * 64 + 64]

    def odd_pack(h):
        @pl.loop(0, N, unroll=2)
        def _(b):
            for a in range(3):
                st2[h, b, a] = tout[a, pl.ds(b * 64, 64)].astype(BF16).reshape(2, W, DH)

    outs = []

    def put(src, dst):
        c = pltpu.make_async_copy(src, dst, osem.at[len(outs)])
        c.start()
        outs.append(c)

    def even_out():
        for h in range(2):
            for a, acc in ((1, acck), (2, accv)):
                for r in range(2):
                    part = acc[h, (1 + r) * C : (2 + r) * C]
                    part = part * SCALE if a == 1 else part
                    oe[h, a, r] = part.astype(BF16).reshape(N, W, DH)
            put(oe.at[h], ev.at[h])

    for h in range(2):
        mine = pltpu.make_async_copy(st.at[h, me], rc.at[h, me], lsem.at[32 + h])
        mine.start()
        mine.wait()
        for c in sent[h]:
            c.wait_recv()
        odd_head(h)
        if h == 0:
            odd_pack(0)
            put(st2.at[0, me], rc2.at[0, me])
            for j in range(N - 1):
                send_back(0, j)

    for a in range(2):
        for hh in range(4):
            part = accp[a, hh] * SCALE if a == 0 else accp[a, hh]
            at = (a * 4 + hh) * 4
            pgs[at : at + 4] = part.astype(BF16).reshape(4, 16, DH)
    scat = []
    for j, to in enumerate(ids):
        scat.append(remote(pgs.at[to], prs.at[me], pss.at[j], prr.at[j], to))
    odd_pack(1)
    put(st2.at[1, me], rc2.at[1, me])
    for j in range(HALF):
        send_back(1, j)
    prs[me] = pgs[me]
    for c in scat:
        c.wait_recv()
    tot = prs[0].astype(F32)
    for j in range(1, N):
        tot = tot + prs[j].astype(F32)
    psum[...] = tot.astype(BF16)
    put(psum, pag.at[me])
    gath = []
    for j, to in enumerate(ids):
        gath.append(remote(psum, pag.at[me], pas.at[j], par.at[j], to))
    for j in range(HALF, N - 1):
        send_back(1, j)
    stats.wait_recv()
    next_row()
    even_out()

    for h in range(2):
        for c in sent2[h]:
            c.wait_recv()
    for c in gath:
        c.wait_recv()
    for c in outs:
        c.wait()
    for c in sent[0] + sent[1] + [stats] + sent2[0] + sent2[1] + scat + gath:
        c.wait_send()


def merge(ev, od, pag, dq, dk, dv, pkg, pvg):
    for a, out in enumerate((dq, dk, dv)):
        for h in range(2):
            out[:, 2 * h * DH : (2 * h + 1) * DH] = ev[h, a, 0].reshape(-1, DH)
            out[:, (2 * h + 1) * DH : (2 * h + 2) * DH] = od[h, :, a, 0].reshape(-1, DH)
    for a, out in enumerate((pkg, pvg)):
        for hh in range(4):
            at = (a * 4 + hh) * 4
            out[:, hh * DH : (hh + 1) * DH] = pag[at : at + 4].reshape(NPRE, DH).astype(F32)


def body(queries, key_field, value_field, out_grad, prefix_keys, prefix_values):
    grid = (2, N, W, 4 * DH)
    anyspace = pl.BlockSpec(memory_space=pl.ANY)
    vm = pl.BlockSpec(memory_space=pltpu.VMEM)
    dma = pltpu.SemaphoreType.DMA
    ev, od, pag = pl.pallas_call(
        kernel,
        name="strided_backward",
        out_shape=(
            jax.ShapeDtypeStruct((2, 3, 2, N, W, DH), BF16),
            jax.ShapeDtypeStruct((2, N, 3, 2, W, DH), BF16),
            jax.ShapeDtypeStruct((N, 16, DH), BF16),
        ),
        in_specs=[anyspace] * 4 + [vm] * 2,
        out_specs=[anyspace] * 3,
        scratch_shapes=[
            pltpu.VMEM((2, N, 4, 2, W, DH), BF16),
            pltpu.VMEM((2, N, 4, 2, W, DH), BF16),
            pltpu.VMEM((2, 2, N, W, DH), BF16),
            pltpu.VMEM((2, 2, N, W, DH), BF16),
            pltpu.VMEM((2, 3, N, W, DH), BF16),
            pltpu.VMEM((2, 3, N, W, DH), BF16),
            pltpu.VMEM((2, N, W, DH), BF16),
            pltpu.VMEM((2, N, W, DH), BF16),
            pltpu.VMEM((4, NPRE, DH), BF16),
            pltpu.VMEM((4, NPRE, DH), BF16),
            pltpu.VMEM((2, 3 * C, DH), F32),
            pltpu.VMEM((2, 3 * C, DH), F32),
            pltpu.VMEM((2, 4, NPRE, DH), F32),
            pltpu.VMEM((2, 3, 2, N, W, DH), BF16),
            pltpu.VMEM((2, 8, QB), F32),
            pltpu.VMEM((2, 8, QB), F32),
            pltpu.VMEM((4, 2 * C + W, DH), F32),
            pltpu.VMEM((3, 2 * C + W, DH), F32),
            pltpu.VMEM((2, N, 3, 2, W, DH), BF16),
            pltpu.VMEM((N, 16, DH), BF16),
            pltpu.VMEM((N, 16, DH), BF16),
            pltpu.VMEM((16, DH), BF16),
            dma((34,)),
            dma((2, N - 1)), dma((2, N - 1)),
            dma((8,)), dma((8,)), dma((1,)), dma((1,)),
            dma((2, N - 1)), dma((2, N - 1)),
            dma((N - 1,)), dma((N - 1,)), dma((N - 1,)), dma((N - 1,)),
            dma((5,)),
        ],
        compiler_params=pltpu.CompilerParams(
            collective_id=0, has_side_effects=True, vmem_limit_bytes=60 << 20
        ),
    )(
        *[a.reshape(grid) for a in (queries, key_field, value_field, out_grad)],
        prefix_keys,
        prefix_values,
    )
    steps = 2
    wide = pl.BlockSpec((2 * C // steps, 4 * DH), lambda p: (p, 0))
    pre = pl.BlockSpec((NPRE, 4 * DH), lambda p: (0, 0))
    big = jax.ShapeDtypeStruct((2 * C, 4 * DH), BF16)
    small = jax.ShapeDtypeStruct((NPRE, 4 * DH), F32)
    blk = 2 * N // steps
    half = steps // 2
    return pl.pallas_call(
        merge,
        name="merge_heads",
        grid=(steps,),
        out_shape=(big, big, big, small, small),
        in_specs=[
            pl.BlockSpec((2, 3, 1, blk, W, DH), lambda p: (0, 0, p // half, p % half, 0, 0)),
            pl.BlockSpec((2, blk, 3, 1, W, DH), lambda p: (0, p % half, 0, p // half, 0, 0)),
            pl.BlockSpec((N, 16, DH), lambda p: (0, 0, 0)),
        ],
        out_specs=[wide] * 3 + [pre] * 2,
        compiler_params=pltpu.CompilerParams(vmem_limit_bytes=60 << 20),
    )(ev, od, pag)


def solution(mesh):
    split = P("seq", "head")
    shared = P(None, "head")
    return jax.shard_map(
        body,
        mesh=mesh,
        in_specs=(split, split, split, split, shared, shared),
        out_specs=(split, split, split, shared, shared),
        check_vma=False,
    )
```
